768 devices in a mesh: wide: 64 (over y, x, core), narrow: 12 (over z).
Axes of the slice: x: 4, y: 8, z: 12, core: 2. Of those that a mesh axis runs over, the one named last changes fastest.
Arguments:
- start_field: float32 [64, 393216], P(None, ('wide', 'narrow')), may hold values from -6 to 6
- right_side: float32 [64, 393216], P(None, ('wide', 'narrow')), may hold values from -6 to 6
- element_scale: float32 [393216], P(('wide', 'narrow')), may hold values from 2 to 6
- face_scale: float32 [6, 393216], P(None, ('wide', 'narrow')), may hold values from 0.1 to 0.6
- face_nbr: int32 [6, 393216], P(None, ('wide', 'narrow')), may hold values from -1 to 767, as said below
- send_list: int32 [4, 49152], P(None, ('wide', 'narrow')), may hold values from 0 to 511, as said below
- counts: int32 [768], P(('wide', 'narrow')), may hold values from 256 to 512, as said below
- coarse_slot: int32 [393216], P(('wide', 'narrow')), may hold values from 0 to 511, as said below
- elem_block: float32 [64, 64], replicated, may hold values from -1.5 to 1.5
- smooth_block: float32 [64, 64], replicated, may hold values from -1.5 to 1.5
- face_blocks: float32 [6, 64, 64], replicated, may hold values from -0.375 to 0.375
- prolong: float32 [8, 64, 8], replicated, may hold values from -1 to 1
- coarse_scale: float32 [49152], P(('wide', 'narrow')), may hold values from 2 to 6
- coarse_face_scale: float32 [6, 49152], P(None, ('wide', 'narrow')), may hold values from 0.1 to 0.6
- coarse_nbr: int32 [6, 49152], P(None, ('wide', 'narrow')), may hold values from -1 to 127, as said below
- coarse_send: int32 [4, 12288], P(None, ('wide', 'narrow')), may hold values from 0 to 63, as said below
- coarse_block: float32 [8, 8], replicated, may hold values from -1.5 to 1.5
- coarse_smooth: float32 [8, 8], replicated, may hold values from -1.5 to 1.5
- coarse_faces: float32 [6, 8, 8], replicated, may hold values from -0.9 to 0.9
Outputs:
- smoothed_field: float32 [64, 393216], P(None, ('wide', 'narrow'))
- coarse_correction: float32 [8, 49152], P(None, ('wide', 'narrow'))
The draws below stay inside these ranges and needn't reach their ends.
Inputs may be any that keep to these rules, and one draw needn't show every extreme that they name: `face_nbr`: -1 marks a face without neighbour; a value below 512 names a slot of the same partition; 512 + d * 64 + j names the j-th element sent by the neighbouring partition in direction d. Each partition names every value from 512 to 767 on some face. `send_list`: row d holds, for each partition, 64 distinct local slots: row 0 goes to the partition one higher on wide, row 1 one lower on wide, rows 2 and 3 likewise on narrow, cyclically. `counts`: one partition has 512 active elements and one has 256. `coarse_slot`: within each partition a permutation of 0 to 511. `coarse_nbr`: as face_nbr, with 64 coarse elements and 16 sent in each direction. `coarse_send`: as send_list, 16 distinct local coarse elements for each partition and direction.
All inputs are finite; a program needn't handle non-finite values.
Results may differ from the reference program's by a relative error of at most 0.0003.
Values sent between devices are 32-bit elements; how exact they have to be, the bound alone decides.
A program may use at most 32 MiB of HBM per device.

```python
import math
import jax
import jax.numpy as jnp
from jax import lax

DOF = 64
CDOF = 8
E = 512
CS = 3
B = 64
NC = 64
SB = 16
PW = 64
PN = 12
DEVS = 768
NELEM = 393216
NCTOT = 49152


def neighbour_table(key, local_count, send_count):
    total = local_count * DEVS
    key_kind, key_near, key_far, key_cover = jax.random.split(key, 4)
    kinds = jax.random.randint(key_kind, (6, total), 0, 20)
    nearby = jax.random.randint(key_near, (6, total), 0, local_count)
    remote = jax.random.randint(key_far, (6, total), local_count, local_count + 4 * send_count)
    table = jnp.where(kinds < 3, remote, jnp.where(kinds == 3, -1, nearby))
    cover_keys = jax.random.split(key_cover, DEVS)
    picks = jax.vmap(lambda subkey: jax.random.permutation(subkey, local_count)[:4 * send_count])(cover_keys)
    columns = (jnp.arange(DEVS)[:, None] * local_count + picks).reshape(-1)
    values = jnp.tile(local_count + jnp.arange(4 * send_count), DEVS)
    table = table.at[5, columns].set(values)
    return table.astype(jnp.int32)


def send_table(key, local_count, send_count):
    keys = jax.random.split(key, 4 * DEVS)
    picks = jax.vmap(lambda subkey: jax.random.permutation(subkey, local_count)[:send_count])(keys)
    return picks.reshape(4, DEVS * send_count).astype(jnp.int32)


def dominant(key, order, spread):
    key_diag, key_off = jax.random.split(key)
    diagonal = jax.random.uniform(key_diag, (order,), jnp.float32, 0.8, 1.2)
    offdiag = jnp.clip(jax.random.normal(key_off, (order, order), jnp.float32), -4.0, 4.0) * spread
    identity = jnp.eye(order, dtype=jnp.float32)
    return (offdiag * (1.0 - identity) + identity * diagonal[None, :]).astype(jnp.float32)


def draw_face_nbr(key, part):
    return neighbour_table(jax.random.fold_in(key, 11), E, B)


def draw_send_list(key, part):
    return send_table(jax.random.fold_in(key, 12), E, B)


def draw_coarse_nbr(key, part):
    return neighbour_table(jax.random.fold_in(key, 13), NC, SB)


def draw_coarse_send(key, part):
    return send_table(jax.random.fold_in(key, 14), NC, SB)


def draw_counts(key, part):
    key_count, key_order = jax.random.split(jax.random.fold_in(key, 15))
    values = jax.random.randint(key_count, (DEVS,), E // 2, E + 1)
    order = jax.random.permutation(key_order, DEVS)
    values = values.at[order[0]].set(E).at[order[1]].set(E // 2)
    return values.astype(jnp.int32)


def draw_coarse_slot(key, part):
    keys = jax.random.split(jax.random.fold_in(key, 16), DEVS)
    picks = jax.vmap(lambda subkey: jax.random.permutation(subkey, E))(keys)
    return picks.reshape(-1).astype(jnp.int32)


def draw_elem_block(key, part):
    return dominant(jax.random.fold_in(key, 21), DOF, 0.04)


def draw_smooth_block(key, part):
    return dominant(jax.random.fold_in(key, 22), DOF, 0.04)


def draw_coarse_block(key, part):
    return dominant(jax.random.fold_in(key, 23), CDOF, 0.12)


def draw_coarse_smooth(key, part):
    return dominant(jax.random.fold_in(key, 24), CDOF, 0.12)


def shard_levels(key, dims, cuts, least, largest):
    def one(dim, shards_of):
        heights = jax.random.uniform(jax.random.fold_in(jax.random.fold_in(key, 6), dim), (shards_of,), jnp.float32, least / len(cuts), largest / len(cuts))
        return jnp.repeat(jnp.exp(heights), dims[dim] // shards_of).reshape((-1,) + (1,) * (len(dims) - dim - 1))

    loudness = one(*cuts[0])
    for cut in cuts[1:]:
        loudness = loudness * one(*cut)
    return loudness


def scatter_about(stream_key, dims, scale, bound, cuts=(), kind=jnp.bfloat16):
    loudness = shard_levels(stream_key, dims, cuts, -0.22, 0.18) if cuts else 1.0
    values = jax.random.normal(stream_key, dims, jnp.float32) * scale * loudness
    return jnp.minimum(jnp.maximum(values, -bound), bound).astype(kind)


def setup_inputs(seed: int = 0) -> dict:
    arg_keys = jax.random.split(jax.random.key(seed), 20)
    return {
        "start_field": scatter_about(arg_keys[0], (DOF, NELEM), 1.0, 6.0, ((1, 768),), jnp.float32),
        "right_side": scatter_about(arg_keys[1], (DOF, NELEM), 1.0, 6.0, ((1, 768),), jnp.float32),
        "element_scale": jnp.clip(jnp.exp(math.log(6.0) - 1.0986123 * jax.random.uniform(arg_keys[2], (NELEM,), jnp.float32) ** shard_levels(arg_keys[2], (NELEM,), ((0, 768),), -0.2, 0.2)), 2.0, 6.0),
        "face_scale": jnp.clip(jnp.exp(math.log(0.6) - 1.7917595 * jax.random.uniform(arg_keys[3], (6, NELEM), jnp.float32) ** shard_levels(arg_keys[3], (6, NELEM), ((1, 768),), -0.2, 0.2)), 0.1, 0.6),
        "face_nbr": draw_face_nbr(jax.random.fold_in(arg_keys[19], 71), 0),
        "send_list": draw_send_list(jax.random.fold_in(arg_keys[19], 71), 0),
        "counts": draw_counts(jax.random.fold_in(arg_keys[19], 71), 0),
        "coarse_slot": draw_coarse_slot(jax.random.fold_in(arg_keys[19], 71), 0),
        "elem_block": draw_elem_block(jax.random.fold_in(arg_keys[19], 71), 0),
        "smooth_block": draw_smooth_block(jax.random.fold_in(arg_keys[19], 71), 0),
        "face_blocks": scatter_about(arg_keys[10], (6, DOF, DOF), 0.0625, 0.375, (), jnp.float32),
        "prolong": scatter_about(arg_keys[11], (8, DOF, CDOF), 32 ** -0.5, 1.0, (), jnp.float32),
        "coarse_scale": jnp.clip(jnp.exp(math.log(6.0) - 1.0986123 * jax.random.uniform(arg_keys[12], (NCTOT,), jnp.float32) ** shard_levels(arg_keys[12], (NCTOT,), ((0, 768),), -0.2, 0.2)), 2.0, 6.0),
        "coarse_face_scale": jnp.clip(jnp.exp(math.log(0.6) - 1.7917595 * jax.random.uniform(arg_keys[13], (6, NCTOT), jnp.float32) ** shard_levels(arg_keys[13], (6, NCTOT), ((1, 768),), -0.2, 0.2)), 0.1, 0.6),
        "coarse_nbr": draw_coarse_nbr(jax.random.fold_in(arg_keys[19], 71), 0),
        "coarse_send": draw_coarse_send(jax.random.fold_in(arg_keys[19], 71), 0),
        "coarse_block": draw_coarse_block(jax.random.fold_in(arg_keys[19], 71), 0),
        "coarse_smooth": draw_coarse_smooth(jax.random.fold_in(arg_keys[19], 71), 0),
        "coarse_faces": scatter_about(arg_keys[18], (6, CDOF, CDOF), 0.15, 0.9, (), jnp.float32),
    }


OMEGA = 0.7
COARSE_OMEGA = 0.6
HIGH = lax.Precision.HIGHEST


def product(left, right):
    return jnp.dot(left, right, preferred_element_type=jnp.float32, precision=HIGH)


def neighbour_index(table, sends, local_count, send_count):
    total = table.shape[1]
    element = jnp.arange(total, dtype=jnp.int32)
    owner = element // local_count
    wide_pos = owner // PN
    narrow_pos = owner % PN
    sources = jnp.stack([((wide_pos - 1) % PW) * PN + narrow_pos,
                         ((wide_pos + 1) % PW) * PN + narrow_pos,
                         wide_pos * PN + (narrow_pos - 1) % PN,
                         wide_pos * PN + (narrow_pos + 1) % PN])
    targets = []
    for face_index in range(6):
        entry = table[face_index]
        ghost = jnp.clip(entry - local_count, 0, 4 * send_count - 1)
        direction = ghost // send_count
        offset = ghost % send_count
        source = jnp.take_along_axis(sources, direction[None, :], axis=0)[0]
        remote = sends[direction, source * send_count + offset]
        target = jnp.where(entry < local_count, owner * local_count + entry, source * local_count + remote)
        targets.append(jnp.where(entry < 0, -1, target))
    return jnp.stack(targets).astype(jnp.int32)


def apply_operator(current, scale, face_scale, table, block, faces):
    result = scale[None, :] * product(block, current)
    for face_index in range(6):
        target = table[face_index]
        weight = jnp.where(target >= 0, face_scale[face_index], 0.0)
        gathered = jnp.take(current, jnp.maximum(target, 0), axis=1)
        result = result + weight[None, :] * product(faces[face_index], gathered)
    return result


def smooth_step(current, residual, active, scale, block):
    return current + OMEGA * active[None, :] * product(block, residual) / scale[None, :]


def reference(start_field, right_side, element_scale, face_scale, face_nbr, send_list, counts, coarse_slot,
              elem_block, smooth_block, face_blocks, prolong, coarse_scale, coarse_face_scale, coarse_nbr,
              coarse_send, coarse_block, coarse_smooth, coarse_faces):
    rows = start_field.shape[0]
    total = start_field.shape[1]
    element = jnp.arange(total, dtype=jnp.int32)
    owner = element // E
    active = ((element % E) < counts[owner]).astype(jnp.float32)
    fine_index = neighbour_index(face_nbr, send_list, E, B)
    coarse_index = neighbour_index(coarse_nbr, coarse_send, NC, SB)
    start = start_field * active[None, :]
    source = right_side * active[None, :]

    def fine_apply(current):
        return apply_operator(current, element_scale, face_scale, fine_index, elem_block, face_blocks)

    def coarse_apply(current):
        return apply_operator(current, coarse_scale, coarse_face_scale, coarse_index, coarse_block, coarse_faces)

    first_residual = source - fine_apply(start)
    smoothed = smooth_step(start, first_residual, active, element_scale, smooth_block)
    fine_residual = source - fine_apply(smoothed)
    slots = (owner * E + coarse_slot).astype(jnp.int32)
    ordered = jnp.zeros_like(fine_residual).at[:, slots].set(fine_residual)
    ordered = ordered.reshape(rows, total // 8, 8)
    coarse_rhs = jnp.einsum("kij,ick->jc", prolong, ordered, precision=HIGH)
    correction = COARSE_OMEGA * product(coarse_smooth, coarse_rhs) / coarse_scale[None, :]
    for sweep_index in range(CS - 1):
        correction = correction + COARSE_OMEGA * product(coarse_smooth, coarse_rhs - coarse_apply(correction)) / coarse_scale[None, :]
    expanded = jnp.einsum("kij,jc->ick", prolong, correction, precision=HIGH).reshape(rows, total)
    corrected = smoothed + active[None, :] * jnp.take(expanded, slots, axis=1)
    final_residual = source - fine_apply(corrected)
    smoothed_field = smooth_step(corrected, final_residual, active, element_scale, smooth_block)
    return smoothed_field, correction
```

```python
import functools

import jax
import jax.numpy as jnp
from jax import lax
from jax.experimental import pallas as pl
from jax.experimental.pallas import tpu as pltpu
from jax.sharding import PartitionSpec as P

OMEGA = 0.7
COARSE_OMEGA = 0.6
HIGH = lax.Precision.HIGHEST
F32 = jnp.float32
BF16 = jnp.bfloat16
FACES = 6
GROUPS = 4
NT = (((1,), (1,)), ((), ()))


def take(values, lanes):
    return jnp.take_along_axis(values, lanes, axis=1, mode="promise_in_bounds")


def halves(x):
    high = x.astype(BF16).astype(F32)
    return high, x - high


def exact_dot(a, b):
    return jnp.dot(a, b, preferred_element_type=F32, precision=HIGH)


def stack_left(a):
    high, low = halves(a)
    return jnp.concatenate([high, low, high], axis=1).astype(BF16)


def stack_right(b):
    high, low = halves(b)
    high = high.astype(BF16)
    return jnp.concatenate([high, high, low.astype(BF16)], axis=0)


def bf_dot(a, b):
    return jnp.dot(a, b, preferred_element_type=F32)


def kernel(
    wide,
    narrow,
    start_ref,
    right_ref,
    scale_ref,
    face_scale_ref,
    nbr_ref,
    send_ref,
    counts_ref,
    slot_ref,
    elem_ref,
    smooth_ref,
    faces_ref,
    prolong_ref,
    cscale_ref,
    cface_scale_ref,
    cnbr_ref,
    csend_ref,
    cblock_ref,
    csmooth_ref,
    cfaces_ref,
    out_ref,
    corr_ref,
    x_ref,
    sm_ref,
    n_ref,
    y_ref,
    lhs_s,
    lhs_p,
    lhs_sp,
    comp_s,
    comp_p,
    final_ref,
    d_hi,
    d_lo,
    base_ref,
    t_ref,
    coef_ref,
    onehot_ref,
    codes_ref,
    pack1,
    ghost1,
    pack2,
    ghost2,
    q3,
    r3,
    q4,
    r4,
    q5,
    r5,
    send_sem,
    recv_sem,
):
    me_w = lax.axis_index("wide")
    me_n = lax.axis_index("narrow")
    targets = (
        {"wide": lax.rem(me_w + 1, wide), "narrow": me_n},
        {"wide": lax.rem(me_w + wide - 1, wide), "narrow": me_n},
        {"wide": me_w, "narrow": lax.rem(me_n + 1, narrow)},
        {"wide": me_w, "narrow": lax.rem(me_n + narrow - 1, narrow)},
    )
    barrier = pltpu.get_barrier_semaphore()
    for target in targets:
        pl.semaphore_signal(
            barrier, inc=1, device_id=target, device_id_type=pl.DeviceIdType.MESH
        )

    lane = lax.broadcasted_iota(jnp.int32, (8, 128), 1)
    lane1 = lax.broadcasted_iota(jnp.int32, (1, 128), 1)
    low32 = jnp.broadcast_to(lane1 < 64, (32, 128))
    element = lax.broadcasted_iota(jnp.int32, (1, 512), 1)
    active = jnp.where(element < counts_ref[0], 1.0, 0.0).astype(F32)

    def copies(step, sources, buffers):
        return [
            pltpu.make_async_remote_copy(
                src_ref=sources[d],
                dst_ref=buffers.at[d],
                send_sem=send_sem.at[step, d],
                recv_sem=recv_sem.at[step, d],
                device_id=targets[d],
                device_id_type=pl.DeviceIdType.MESH,
            )
            for d in range(4)
        ]

    def start_all(group):
        for d in (2, 3, 0, 1):
            group[d].start()

    def pack(field_ref, packets, codes=None):
        for pair in range(2):
            row = jnp.concatenate(
                [send_ref[2 * pair : 2 * pair + 1, :], send_ref[2 * pair + 1 : 2 * pair + 2, :]],
                axis=1,
            )
            index = jnp.broadcast_to(row & 127, (64, 128))
            group = jnp.broadcast_to(row >> 7, (64, 128))
            picked = jnp.zeros((64, 128), F32)
            for s in range(GROUPS):
                got = take(field_ref[:, s * 128 : (s + 1) * 128], index)
                picked = jnp.where(group == s, got, picked)
            moved = pltpu.roll(picked[32:], 64, 1)
            packets[2 * pair, 0:32, :] = jnp.where(low32, picked[:32], moved)
            packets[2 * pair + 1, 0:32, :] = jnp.where(low32, moved, picked[:32])
            if codes is not None:
                picked = jnp.zeros((8, 128), F32)
                for s in range(GROUPS):
                    got = take(
                        jnp.broadcast_to(codes[:, s * 128 : (s + 1) * 128], (8, 128)),
                        index[:8],
                    )
                    picked = jnp.where(group[:8] == s, got, picked)
                packets[2 * pair, 32:40, :] = picked
                packets[2 * pair + 1, 32:40, :] = picked

    def unpack(ghosts):
        columns = []
        for pair in range(2):
            a = ghosts[2 * pair, 0:32, :]
            b = ghosts[2 * pair + 1, 0:32, :]
            first = jnp.where(low32, a, b)
            second = pltpu.roll(jnp.where(low32, b, a), 64, 1)
            columns.append(jnp.concatenate([first, second], axis=0))
        return jnp.concatenate(columns, axis=1)

    def gather_faces(groups, fresh):
        for t in range(GROUPS):
            span = slice(t * 128, (t + 1) * 128)
            total = jnp.zeros((64, 128), F32) if fresh else n_ref[:, span]
            for f in range(FACES):
                row = nbr_ref[f : f + 1, span]
                index = jnp.broadcast_to(row & 127, (64, 128))
                group = jnp.broadcast_to(row >> 7, (64, 128))
                picked = jnp.zeros((64, 128), F32)
                for s in groups:
                    got = take(
                        y_ref[(f + 1) * 64 : (f + 2) * 64, s * 128 : (s + 1) * 128], index
                    )
                    picked = jnp.where(group == s, got, picked)
                total = total + face_scale_ref[f : f + 1, span] * picked
            n_ref[:, span] = total

    x_ref[...] = start_ref[...] * active
    codes = jnp.where(active > 0.0, slot_ref[...].astype(F32), -1.0)
    pack(x_ref, pack1, codes)
    pl.semaphore_wait(barrier, 4)
    first = copies(0, [pack1.at[d] for d in range(4)], ghost1)
    start_all(first)

    smooth = smooth_ref[...]
    csmooth = csmooth_ref[...]
    prolong_t = prolong_ref[...]
    for f in range(FACES + 1):
        block = elem_ref[...] if f == 0 else faces_ref[f - 1]
        comp_s[f * 64 : (f + 1) * 64, :] = exact_dot(smooth, block)
    lhs_s[...] = stack_left(comp_s[...])
    y_ref[:, :512] = bf_dot(lhs_s[...], stack_right(x_ref[...]))
    gather_faces(range(GROUPS), True)
    row_blocks = lax.broadcasted_iota(jnp.int32, (64, 64), 0) >> 3
    column_blocks = lax.broadcasted_iota(jnp.int32, (64, 64), 1) >> 3
    tiled = jnp.concatenate([csmooth] * 8, axis=1)
    tiled = jnp.concatenate([tiled] * 8, axis=0)
    diagonal = jnp.where(row_blocks == column_blocks, tiled, 0.0)
    restrict = exact_dot(diagonal, prolong_t)
    lhs_sp[...] = stack_left(jnp.concatenate([smooth, restrict], axis=0))
    t_ref[...] = bf_dot(lhs_sp[...], stack_right(right_ref[...]))
    inverse = 1.0 / scale_ref[...]
    omega = OMEGA * active

    for copy in first:
        copy.wait_recv()
    y_ref[64:, 512:] = bf_dot(lhs_s[64:, :], stack_right(unpack(ghost1)))
    gather_faces((4, 5), False)
    sm_ref[:, :512] = x_ref[...] + omega * ((t_ref[:64] - n_ref[...]) * inverse - y_ref[:64, :512])
    pack(sm_ref, pack2)
    second = copies(1, [pack2.at[d] for d in range(4)], ghost2)
    start_all(second)

    for f in range(FACES + 1):
        block = elem_ref[...] if f == 0 else faces_ref[f - 1]
        comp_p[f * 64 : (f + 1) * 64, :] = exact_dot(restrict, block)
    lhs_p[...] = stack_left(comp_p[...])
    y_ref[:, :512] = bf_dot(lhs_p[...], stack_right(sm_ref[:, :512]))
    gather_faces(range(GROUPS), True)
    n_ref[...] = active * t_ref[64:] - scale_ref[...] * y_ref[:64, :512] - n_ref[...]
    together = jnp.concatenate([cblock_ref[...]] + [cfaces_ref[f] for f in range(FACES)], axis=1)
    coarse = exact_dot(csmooth, together)
    for c in range(8 * (FACES + 1)):
        coef_ref[c] = jnp.broadcast_to(coarse[:, c : c + 1], (8, 128))
    parent = slot_ref[...] >> 3
    child = slot_ref[...] & 7
    row128 = lax.broadcasted_iota(jnp.int32, (128, 512), 0) & 63
    onehot_ref[...] = jnp.where(row128 == parent, 1.0, 0.0).astype(BF16)
    cinv = COARSE_OMEGA / jnp.concatenate([cscale_ref[...]] * 2, axis=1)
    cnbr = jnp.concatenate([cnbr_ref[...]] * 2, axis=1)
    cweight = jnp.concatenate([cface_scale_ref[...]] * 2, axis=1)
    cweight = jnp.where(cnbr >= 0, cweight, 0.0) * cinv
    clane = jnp.maximum(cnbr, 0)
    csend = csend_ref[...]
    row = jnp.concatenate([csend[d : d + 1] for d in range(4)] * 2, axis=1)
    qlane = jnp.broadcast_to(row, (8, 128))

    for copy in second:
        copy.wait_recv()
    sm_ref[:, 512:] = unpack(ghost2)
    y_ref[64:, 512:] = bf_dot(lhs_p[64:, :], stack_right(sm_ref[:, 512:]))

    def minus_faces():
        for t in range(GROUPS):
            span = slice(t * 128, (t + 1) * 128)
            total = n_ref[:, span]
            for f in range(FACES):
                row = nbr_ref[f : f + 1, span]
                index = jnp.broadcast_to(row & 127, (64, 128))
                group = jnp.broadcast_to(row >> 7, (64, 128))
                picked = jnp.zeros((64, 128), F32)
                for s in (4, 5):
                    got = take(
                        y_ref[(f + 1) * 64 : (f + 2) * 64, s * 128 : (s + 1) * 128], index
                    )
                    picked = jnp.where(group == s, got, picked)
                total = total - face_scale_ref[f : f + 1, span] * picked
            n_ref[:, span] = total

    minus_faces()
    chosen = jnp.zeros((8, 512), F32)
    for k in range(8):
        chosen = jnp.where(child == k, n_ref[8 * k : 8 * k + 8, :], chosen)
    high, low = halves(chosen)
    both = jnp.concatenate([high, low], axis=0).astype(BF16)
    summed = lax.dot_general(both, onehot_ref[...], NT, preferred_element_type=F32)
    base_c = (summed[:8] + summed[8:]) * cinv

    def extend(own, received):
        ext = own
        for d in range(4):
            here = (lane >= 64 + 16 * d) & (lane < 80 + 16 * d)
            ext = jnp.where(here, received[d], ext)
        return ext

    def sweep(own, ext):
        rows = [jnp.broadcast_to(ext[j : j + 1, :], (8, 128)) for j in range(8)]
        total = None
        for f in range(FACES + 1):
            product = coef_ref[8 * f] * rows[0]
            for j in range(1, 8):
                product = product + coef_ref[8 * f + j] * rows[j]
            if f == 0:
                total = COARSE_OMEGA * product
            else:
                index = jnp.broadcast_to(clane[f - 1 : f], (8, 128))
                total = total + cweight[f - 1 : f] * take(product, index)
        return own + base_c - total

    q3[...] = take(base_c, qlane)
    third = copies(2, [q3] * 4, r3)
    start_all(third)

    y_ref[...] = bf_dot(lhs_s[...], stack_right(sm_ref[...]))
    gather_faces(range(GROUPS), True)
    eye = jnp.where(
        lax.broadcasted_iota(jnp.int32, (64, 64), 0) == lax.broadcasted_iota(jnp.int32, (64, 64), 1),
        1.0,
        0.0,
    )
    left = jnp.concatenate([eye - OMEGA * comp_s[:64], comp_s[64:]], axis=0)
    products = lax.dot_general(left, prolong_t, NT, preferred_element_type=F32, precision=HIGH)
    wide_products = jnp.concatenate(
        [products[f * 64 : (f + 1) * 64] for f in range(FACES + 1)], axis=1
    )
    high, low = halves(wide_products)
    final_ref[...] = jnp.concatenate([high, low], axis=0).astype(BF16)

    for copy in third:
        copy.wait_recv()
    c1 = sweep(base_c, extend(base_c, r3))
    q4[...] = take(c1, qlane)
    fourth = copies(3, [q4] * 4, r4)
    start_all(fourth)

    gather_faces((4, 5), False)
    base_ref[...] = sm_ref[:, :512] + omega * (
        (t_ref[:64] - n_ref[...]) * inverse - y_ref[:64, :512]
    )
    code_groups = [
        jnp.broadcast_to(codes[:, s * 128 : (s + 1) * 128], (8, 128)) for s in range(GROUPS)
    ]
    for pair in range(2):
        a = ghost1[2 * pair, 32:40, :]
        b = ghost1[2 * pair + 1, 32:40, :]
        a = jnp.where(a >= 0.0, a + 512.0 * (2 * pair + 1), -1.0)
        b = jnp.where(b >= 0.0, b + 512.0 * (2 * pair + 2), -1.0)
        code_groups.append(jnp.where(lane < 64, a, b))
    for t in range(GROUPS):
        span = slice(t * 128, (t + 1) * 128)
        table = jnp.concatenate([nbr_ref[:, span], jnp.full((2, 128), -1, jnp.int32)], axis=0)
        index = table & 127
        group = table >> 7
        picked = jnp.full((8, 128), -1.0, F32)
        for s in range(GROUPS + 2):
            picked = jnp.where(group == s, take(code_groups[s], index), picked)
        codes_ref[:, span] = picked.astype(jnp.int32)
    codes_ref[6:7, :] = codes.astype(jnp.int32)

    for copy in fourth:
        copy.wait_recv()
    c2 = sweep(c1, extend(c1, r4))
    q5[...] = jnp.where(lane < 64, c2, pltpu.roll(c2, 64, 1))
    fifth = copies(4, [q5] * 4, r5)
    start_all(fifth)
    corr_ref[...] = c2[:, :64]
    for copy in fifth:
        copy.wait_recv()
    sources = (
        jnp.where(lane < 64, c2, r5[0]),
        jnp.where(lane < 64, r5[1], r5[2]),
        r5[3],
    )
    for f in range(FACES + 1):
        for t in range(GROUPS):
            span = slice(t * 128, (t + 1) * 128)
            row = codes_ref[(f + 6) % 7 : (f + 6) % 7 + 1, span]
            index = jnp.broadcast_to((row >> 3) & 127, (8, 128))
            group = jnp.broadcast_to(row >> 10, (8, 128))
            kid = jnp.broadcast_to(row & 7, (8, 128))
            kid = jnp.where(jnp.broadcast_to(row, (8, 128)) < 0, -1, kid)
            picked = jnp.zeros((8, 128), F32)
            for s in range(3 if f else 1):
                picked = jnp.where(group == s, take(sources[s], index), picked)
            if f:
                weight = face_scale_ref[f - 1 : f, span] * (omega * inverse)[:, span]
                picked = -weight * picked
            high, low = halves(picked)
            d_hi[f * 64 : (f + 1) * 64, span] = jnp.concatenate(
                [jnp.where(kid == k, high, 0.0) for k in range(8)], axis=0
            ).astype(BF16)
            d_lo[f * 64 : (f + 1) * 64, span] = jnp.concatenate(
                [jnp.where(kid == k, low, 0.0) for k in range(8)], axis=0
            ).astype(BF16)
    both = bf_dot(final_ref[...], d_hi[...])
    rest = bf_dot(final_ref[:64], d_lo[...])
    out_ref[...] = base_ref[...] + (both[:64] + both[64:] + rest)
    for group in (first, second, third, fourth, fifth):
        for copy in group:
            copy.wait_send()


def body(wide, narrow, *args):
    (
        start_field,
        right_side,
        element_scale,
        face_scale,
        face_nbr,
        send_list,
        counts,
        coarse_slot,
        elem_block,
        smooth_block,
        face_blocks,
        prolong,
        coarse_scale,
        coarse_face_scale,
        coarse_nbr,
        coarse_send,
        coarse_block,
        coarse_smooth,
        coarse_faces,
    ) = args
    vmem = pl.BlockSpec(memory_space=pltpu.VMEM)
    specs = [vmem] * len(args)
    specs[6] = pl.BlockSpec(memory_space=pltpu.SMEM)
    return tuple(
        pl.pallas_call(
            functools.partial(kernel, wide, narrow),
            out_shape=[
                jax.ShapeDtypeStruct((64, 512), F32),
                jax.ShapeDtypeStruct((8, 64), F32),
            ],
            in_specs=specs,
            out_specs=[vmem, vmem],
            scratch_shapes=[
                pltpu.VMEM((64, 512), F32),
                pltpu.VMEM((64, 768), F32),
                pltpu.VMEM((64, 512), F32),
                pltpu.VMEM((448, 768), F32),
                pltpu.VMEM((448, 192), BF16),
                pltpu.VMEM((448, 192), BF16),
                pltpu.VMEM((128, 192), BF16),
                pltpu.VMEM((448, 64), F32),
                pltpu.VMEM((448, 64), F32),
                pltpu.VMEM((128, 448), BF16),
                pltpu.VMEM((448, 512), BF16),
                pltpu.VMEM((448, 512), BF16),
                pltpu.VMEM((64, 512), F32),
                pltpu.VMEM((128, 512), F32),
                pltpu.VMEM((56, 8, 128), F32),
                pltpu.VMEM((128, 512), BF16),
                pltpu.VMEM((8, 512), jnp.int32),
                pltpu.VMEM((4, 40, 128), F32),
                pltpu.VMEM((4, 40, 128), F32),
                pltpu.VMEM((4, 32, 128), F32),
                pltpu.VMEM((4, 32, 128), F32),
                pltpu.VMEM((8, 128), F32),
                pltpu.VMEM((4, 8, 128), F32),
                pltpu.VMEM((8, 128), F32),
                pltpu.VMEM((4, 8, 128), F32),
                pltpu.VMEM((8, 128), F32),
                pltpu.VMEM((4, 8, 128), F32),
                pltpu.SemaphoreType.DMA((5, 4)),
                pltpu.SemaphoreType.DMA((5, 4)),
            ],
            compiler_params=pltpu.CompilerParams(
                collective_id=0, has_side_effects=True, vmem_limit_bytes=32 * 1024 * 1024
            ),
        )(
            start_field,
            right_side,
            element_scale.reshape(1, -1),
            face_scale,
            face_nbr,
            send_list,
            counts,
            coarse_slot.reshape(1, -1),
            elem_block,
            smooth_block,
            face_blocks,
            prolong.transpose(0, 2, 1).reshape(64, 64),
            coarse_scale.reshape(1, -1),
            coarse_face_scale,
            coarse_nbr,
            coarse_send,
            coarse_block,
            coarse_smooth,
            coarse_faces,
        )
    )


def solution(mesh):
    both = ("wide", "narrow")
    split1, split2, whole = P(both), P(None, both), P()
    return jax.shard_map(
        functools.partial(body, mesh.shape["wide"], mesh.shape["narrow"]),
        mesh=mesh,
        in_specs=(
            split2,
            split2,
            split1,
            split2,
            split2,
            split2,
            split1,
            split1,
            whole,
            whole,
            whole,
            whole,
            split1,
            split2,
            split2,
            split2,
            whole,
            whole,
            whole,
        ),
        out_specs=(split2, split2),
        check_vma=False,
    )
```

```python
import functools

import jax
import jax.numpy as jnp
from jax import lax
from jax.experimental import pallas as pl
from jax.experimental.pallas import tpu as pltpu
from jax.sharding import PartitionSpec as P

OMEGA = 0.7
COARSE_OMEGA = 0.6
HIGH = lax.Precision.HIGHEST
F32 = jnp.float32
BF16 = jnp.bfloat16
FACES = 6
GROUPS = 4
NT = (((1,), (1,)), ((), ()))
SOURCES = ((-1, 0), (1, 0), (0, -1), (0, 1))
RANGE = range(-3, 4)
BALL = sorted(
    ((a, b) for a in RANGE for b in RANGE if 0 < abs(a) + abs(b) <= 3),
    key=lambda o: (-abs(o[0]) - abs(o[1]), o),
)
NEAR = ((0, 0),) + SOURCES
NEXT = NEAR + ((-2, 0), (-1, -1), (-1, 1), (2, 0), (1, -1), (1, 1), (0, -2), (0, 2))


def take(values, lanes):
    return jnp.take_along_axis(values, lanes, axis=1, mode="promise_in_bounds")


def halves(x):
    high = x.astype(BF16).astype(F32)
    return high, x - high


def exact_dot(a, b):
    return jnp.dot(a, b, preferred_element_type=F32, precision=HIGH)


def stack_left(a):
    high, low = halves(a)
    return jnp.concatenate([high, low, high], axis=1).astype(BF16)


def stack_right(b):
    high, low = halves(b)
    high = high.astype(BF16)
    return jnp.concatenate([high, high, low.astype(BF16)], axis=0)


def bf_dot(a, b):
    return jnp.dot(a, b, preferred_element_type=F32)


def kernel(
    wide,
    narrow,
    start_hbm,
    right_hbm,
    scale_hbm,
    face_scale_hbm,
    nbr_hbm,
    send_hbm,
    counts_hbm,
    slot_hbm,
    elem_hbm,
    smooth_hbm,
    faces_hbm,
    prolong_hbm,
    cscale_hbm,
    cface_scale_hbm,
    cnbr_hbm,
    csend_hbm,
    cblock_hbm,
    csmooth_hbm,
    cfaces_hbm,
    out_ref,
    corr_ref,
    x_ref,
    sm_ref,
    n_ref,
    y_ref,
    lhs_s,
    lhs_p,
    lhs_sp,
    comp_s,
    comp_p,
    final_ref,
    d_hi,
    d_lo,
    base_ref,
    t_ref,
    coef_ref,
    onehot_ref,
    codes_ref,
    pack1,
    ghost1,
    pack2,
    ghost2,
    pack2n,
    ghost2n,
    tile3,
    ghost3,
    clane_ref,
    cweight_ref,
    qlane_ref,
    send_sem,
    recv_sem,
    send_sem3,
    recv_sem3,
    start_ref,
    right_ref,
    scale_ref,
    face_scale_ref,
    nbr_ref,
    send_ref,
    slot_ref,
    elem_ref,
    smooth_ref,
    faces_ref,
    prolong_ref,
    cscale_ref,
    cface_scale_ref,
    cnbr_ref,
    csend_ref,
    cblock_ref,
    csmooth_ref,
    cfaces_ref,
    counts_ref,
    load_sem,
):
    loads = {
        name: pltpu.make_async_copy(source, target, load_sem.at[i])
        for i, (name, source, target) in enumerate(
            (
                ("send", send_hbm, send_ref),
                ("counts", counts_hbm, counts_ref),
                ("start", start_hbm, start_ref),
                ("slot", slot_hbm, slot_ref),
                ("right", right_hbm, right_ref),
                ("scale", scale_hbm, scale_ref),
                ("face_scale", face_scale_hbm, face_scale_ref),
                ("nbr", nbr_hbm, nbr_ref),
                ("elem", elem_hbm, elem_ref),
                ("smooth", smooth_hbm, smooth_ref),
                ("faces", faces_hbm, faces_ref),
                ("prolong", prolong_hbm, prolong_ref),
                ("cscale", cscale_hbm, cscale_ref),
                ("cface_scale", cface_scale_hbm, cface_scale_ref),
                ("cnbr", cnbr_hbm, cnbr_ref),
                ("csend", csend_hbm, csend_ref),
                ("cblock", cblock_hbm, cblock_ref),
                ("csmooth", csmooth_hbm, csmooth_ref),
                ("cfaces", cfaces_hbm, cfaces_ref),
            )
        )
    }
    for load in loads.values():
        load.start()

    def arrive(*names):
        for name in names:
            loads[name].wait()

    me_w = lax.axis_index("wide")
    me_n = lax.axis_index("narrow")
    targets = (
        {"wide": lax.rem(me_w + 1, wide), "narrow": me_n},
        {"wide": lax.rem(me_w + wide - 1, wide), "narrow": me_n},
        {"wide": me_w, "narrow": lax.rem(me_n + 1, narrow)},
        {"wide": me_w, "narrow": lax.rem(me_n + narrow - 1, narrow)},
    )
    barrier = pltpu.get_barrier_semaphore()
    for target in targets:
        pl.semaphore_signal(
            barrier, inc=1, device_id=target, device_id_type=pl.DeviceIdType.MESH
        )

    lane = lax.broadcasted_iota(jnp.int32, (8, 128), 1)
    lane1 = lax.broadcasted_iota(jnp.int32, (1, 128), 1)
    low32 = jnp.broadcast_to(lane1 < 64, (32, 128))
    element = lax.broadcasted_iota(jnp.int32, (1, 512), 1)
    def copies(step, sources, buffers):
        return [
            pltpu.make_async_remote_copy(
                src_ref=sources[d],
                dst_ref=buffers[d],
                send_sem=send_sem.at[step, d],
                recv_sem=recv_sem.at[step, d],
                device_id=targets[d],
                device_id_type=pl.DeviceIdType.MESH,
            )
            for d in range(4)
        ]

    def start_all(group):
        for d in (2, 3, 0, 1):
            group[d].start()

    def send_row(pair):
        return jnp.concatenate(
            [send_ref[2 * pair : 2 * pair + 1, :], send_ref[2 * pair + 1 : 2 * pair + 2, :]], axis=1
        )

    def pack(field_ref, packets):
        for pair in range(2):
            row = send_row(pair)
            index = jnp.broadcast_to(row & 127, (64, 128))
            group = jnp.broadcast_to(row >> 7, (64, 128))
            picked = jnp.zeros((64, 128), F32)
            for s in range(GROUPS):
                got = take(field_ref[:, s * 128 : (s + 1) * 128], index)
                picked = jnp.where(group == s, got, picked)
            moved = pltpu.roll(picked[32:], 64, 1)
            packets[2 * pair][0:32, :] = jnp.where(low32, picked[:32], moved)
            packets[2 * pair + 1][0:32, :] = jnp.where(low32, moved, picked[:32])

    def unpack(ghosts):
        columns = []
        for pair in range(2):
            a = ghosts[2 * pair][0:32, :]
            b = ghosts[2 * pair + 1][0:32, :]
            first = jnp.where(low32, a, b)
            second = pltpu.roll(jnp.where(low32, b, a), 64, 1)
            columns.append(jnp.concatenate([first, second], axis=0))
        return jnp.concatenate(columns, axis=1)

    def gather_faces(groups, fresh):
        for t in range(GROUPS):
            span = slice(t * 128, (t + 1) * 128)
            total = jnp.zeros((64, 128), F32) if fresh else n_ref[:, span]
            for f in range(FACES):
                row = nbr_ref[f : f + 1, span]
                index = jnp.broadcast_to(row & 127, (64, 128))
                group = jnp.broadcast_to(row >> 7, (64, 128))
                picked = jnp.zeros((64, 128), F32)
                for s in groups:
                    got = take(
                        y_ref[(f + 1) * 64 : (f + 2) * 64, s * 128 : (s + 1) * 128], index
                    )
                    picked = jnp.where(group == s, got, picked)
                total = total + face_scale_ref[f : f + 1, span] * picked
            n_ref[:, span] = total

    arrive("counts", "send", "start", "slot", "cscale", "cface_scale", "cnbr", "csend")
    active = jnp.where(element < counts_ref[0, 0], 1.0, 0.0).astype(F32)
    x_ref[...] = start_ref[...] * active
    codes = jnp.where(active > 0.0, slot_ref[...].astype(F32), -1.0)
    cinv = COARSE_OMEGA / jnp.concatenate([cscale_ref[...]] * 2, axis=1)
    cnbr = cnbr_ref[...]
    weights = jnp.where(cnbr >= 0, cface_scale_ref[...], 0.0) * cinv[:, :64]
    csend = csend_ref[...]
    static = jnp.concatenate(
        [
            jnp.concatenate([jnp.maximum(cnbr, 0).astype(F32), weights], axis=1),
            jnp.concatenate([csend[d : d + 1] for d in range(4)] * 2, axis=1).astype(F32),
        ],
        axis=0,
    )
    pack(x_ref, [pack1.at[d] for d in range(4)])
    for pair in range(2):
        row = send_row(pair)
        index = jnp.broadcast_to(row & 127, (8, 128))
        group = jnp.broadcast_to(row >> 7, (8, 128))
        picked = jnp.zeros((8, 128), F32)
        for s in range(GROUPS):
            span = slice(s * 128, (s + 1) * 128)
            got = take(jnp.broadcast_to(codes[:, span], (8, 128)), index)
            picked = jnp.where(group == s, got, picked)
        tile = jnp.concatenate([static, picked[:1]], axis=0)
        pack1[2 * pair, 32:40, :] = tile
        pack1[2 * pair + 1, 32:40, :] = tile
    pl.semaphore_wait(barrier, 4)
    first = copies(0, [pack1.at[d] for d in range(4)], [ghost1.at[d] for d in range(4)])
    start_all(first)

    arrive("smooth", "elem", "faces", "nbr", "face_scale", "csmooth", "prolong", "right", "scale")
    smooth = smooth_ref[...]
    csmooth = csmooth_ref[...]
    prolong_t = prolong_ref[...]
    for f in range(FACES + 1):
        block = elem_ref[...] if f == 0 else faces_ref[f - 1]
        comp_s[f * 64 : (f + 1) * 64, :] = exact_dot(smooth, block)
    lhs_s[...] = stack_left(comp_s[...])
    y_ref[:, :512] = bf_dot(lhs_s[...], stack_right(x_ref[...]))
    gather_faces(range(GROUPS), True)
    row_blocks = lax.broadcasted_iota(jnp.int32, (64, 64), 0) >> 3
    column_blocks = lax.broadcasted_iota(jnp.int32, (64, 64), 1) >> 3
    tiled = jnp.concatenate([csmooth] * 8, axis=1)
    tiled = jnp.concatenate([tiled] * 8, axis=0)
    diagonal = jnp.where(row_blocks == column_blocks, tiled, 0.0)
    restrict = exact_dot(diagonal, prolong_t)
    lhs_sp[...] = stack_left(jnp.concatenate([smooth, restrict], axis=0))
    t_ref[...] = bf_dot(lhs_sp[...], stack_right(right_ref[...]))
    inverse = 1.0 / scale_ref[...]
    omega = OMEGA * active

    for copy in first:
        copy.wait_recv()
    y_ref[64:, 512:] = bf_dot(lhs_s[64:, :], stack_right(unpack([ghost1.at[d] for d in range(4)])))
    gather_faces((4, 5), False)
    sm_ref[:, :512] = x_ref[...] + omega * ((t_ref[:64] - n_ref[...]) * inverse - y_ref[:64, :512])
    packets2 = [pack2.at[0], pack2.at[1], pack2n.at[0], pack2n.at[1]]
    arrived2 = [ghost2.at[0], ghost2.at[1], ghost2n.at[0], ghost2n.at[1]]
    pack(sm_ref, packets2)
    for d in range(4):
        for i, source in enumerate((d, 2, 3) if d < 2 else (d,)):
            packets2[d][32 + 8 * i : 40 + 8 * i, :] = ghost1[source, 32:40, :]
    second = copies(1, packets2, arrived2)
    start_all(second)

    for f in range(FACES + 1):
        block = elem_ref[...] if f == 0 else faces_ref[f - 1]
        comp_p[f * 64 : (f + 1) * 64, :] = exact_dot(restrict, block)
    lhs_p[...] = stack_left(comp_p[...])
    y_ref[:, :512] = bf_dot(lhs_p[...], stack_right(sm_ref[:, :512]))
    gather_faces(range(GROUPS), True)
    n_ref[...] = active * t_ref[64:] - scale_ref[...] * y_ref[:64, :512] - n_ref[...]
    arrive("cblock", "cfaces")
    together = jnp.concatenate([cblock_ref[...]] + [cfaces_ref[f] for f in range(FACES)], axis=1)
    coarse = exact_dot(csmooth, together)
    for c in range(8 * (FACES + 1)):
        coef_ref[c] = jnp.broadcast_to(coarse[:, c : c + 1], (8, 128))
    parent = slot_ref[...] >> 3
    child = slot_ref[...] & 7
    row128 = lax.broadcasted_iota(jnp.int32, (128, 512), 0) & 63
    onehot_ref[...] = jnp.where(row128 == parent, 1.0, 0.0).astype(BF16)

    def keep_static(i, tile):
        clane_ref[i] = tile.astype(jnp.int32)
        cweight_ref[i] = pltpu.roll(tile, 64, 1)
        qlane_ref[i] = jnp.broadcast_to(tile[6:7], (8, 128)).astype(jnp.int32)

    keep_static(0, pack1[0, 32:40, :])
    for d in range(4):
        keep_static(1 + d, ghost1[d, 32:40, :])

    for copy in second:
        copy.wait_recv()
    sm_ref[:, 512:] = unpack(arrived2)
    y_ref[64:, 512:] = bf_dot(lhs_p[64:, :], stack_right(sm_ref[:, 512:]))

    def minus_faces():
        for t in range(GROUPS):
            span = slice(t * 128, (t + 1) * 128)
            total = n_ref[:, span]
            for f in range(FACES):
                row = nbr_ref[f : f + 1, span]
                index = jnp.broadcast_to(row & 127, (64, 128))
                group = jnp.broadcast_to(row >> 7, (64, 128))
                picked = jnp.zeros((64, 128), F32)
                for s in (4, 5):
                    got = take(
                        y_ref[(f + 1) * 64 : (f + 2) * 64, s * 128 : (s + 1) * 128], index
                    )
                    picked = jnp.where(group == s, got, picked)
                total = total - face_scale_ref[f : f + 1, span] * picked
            n_ref[:, span] = total

    minus_faces()
    chosen = jnp.zeros((8, 512), F32)
    for k in range(8):
        chosen = jnp.where(child == k, n_ref[8 * k : 8 * k + 8, :], chosen)
    high, low = halves(chosen)
    both = jnp.concatenate([high, low], axis=0).astype(BF16)
    summed = lax.dot_general(both, onehot_ref[...], NT, preferred_element_type=F32)
    base_c = (summed[:8] + summed[8:]) * cinv

    def extend(parts, at):
        ext = parts[at]
        for d, (a, b) in enumerate(SOURCES):
            here = (lane >= 64 + 16 * d) & (lane < 80 + 16 * d)
            ext = jnp.where(here, parts[(at[0] + a, at[1] + b)], ext)
        return ext

    def sweep(own, right, ext, i):
        rows = [jnp.broadcast_to(ext[j : j + 1, :], (8, 128)) for j in range(8)]
        total = None
        for f in range(FACES + 1):
            product = coef_ref[8 * f] * rows[0]
            for j in range(1, 8):
                product = product + coef_ref[8 * f + j] * rows[j]
            if f == 0:
                total = COARSE_OMEGA * product
            else:
                index = jnp.broadcast_to(clane_ref[i, f - 1 : f, :], (8, 128))
                total = total + cweight_ref[i, f - 1 : f, :] * take(product, index)
        return own + right - total

    tile3[...] = jnp.where(lane < 64, base_c, take(base_c, qlane_ref[0]))
    third = [
        pltpu.make_async_remote_copy(
            src_ref=tile3,
            dst_ref=ghost3.at[BALL.index((-a, -b))],
            send_sem=send_sem3.at[i],
            recv_sem=recv_sem3.at[BALL.index((-a, -b))],
            device_id={
                "wide": lax.rem(me_w + (a + wide), wide),
                "narrow": lax.rem(me_n + (b + narrow), narrow),
            },
            device_id_type=pl.DeviceIdType.MESH,
        )
        for i, (a, b) in enumerate(BALL)
    ]
    for copy in third:
        copy.start()

    y_ref[...] = bf_dot(lhs_s[...], stack_right(sm_ref[...]))
    gather_faces(range(GROUPS), True)
    eye = jnp.where(
        lax.broadcasted_iota(jnp.int32, (64, 64), 0) == lax.broadcasted_iota(jnp.int32, (64, 64), 1),
        1.0,
        0.0,
    )
    left = jnp.concatenate([eye - OMEGA * comp_s[:64], comp_s[64:]], axis=0)
    products = lax.dot_general(left, prolong_t, NT, preferred_element_type=F32, precision=HIGH)
    wide_products = jnp.concatenate(
        [products[f * 64 : (f + 1) * 64] for f in range(FACES + 1)], axis=1
    )
    high, low = halves(wide_products)
    final_ref[...] = jnp.concatenate([high, low], axis=0).astype(BF16)

    for d in range(2):
        for i in range(3):
            keep_static(5 + 3 * d + i, ghost2[d, 32 + 8 * i : 40 + 8 * i, :])
        keep_static(11 + d, ghost2n[d, 32:40, :])
    gather_faces((4, 5), False)
    base_ref[...] = sm_ref[:, :512] + omega * (
        (t_ref[:64] - n_ref[...]) * inverse - y_ref[:64, :512]
    )
    code_groups = [
        jnp.broadcast_to(codes[:, s * 128 : (s + 1) * 128], (8, 128)) for s in range(GROUPS)
    ]
    for pair in range(2):
        a = jnp.broadcast_to(ghost1[2 * pair, 39:40, :], (8, 128))
        b = jnp.broadcast_to(ghost1[2 * pair + 1, 39:40, :], (8, 128))
        a = jnp.where(a >= 0.0, a + 512.0 * (2 * pair + 1), -1.0)
        b = jnp.where(b >= 0.0, b + 512.0 * (2 * pair + 2), -1.0)
        code_groups.append(jnp.where(lane < 64, a, b))
    for t in range(GROUPS):
        span = slice(t * 128, (t + 1) * 128)
        table = jnp.concatenate([nbr_ref[:, span], jnp.full((2, 128), -1, jnp.int32)], axis=0)
        index = table & 127
        group = table >> 7
        picked = jnp.full((8, 128), -1.0, F32)
        for s in range(GROUPS + 2):
            picked = jnp.where(group == s, take(code_groups[s], index), picked)
        codes_ref[:, span] = picked.astype(jnp.int32)
    codes_ref[6:7, :] = codes.astype(jnp.int32)

    for copy in third:
        copy.wait_recv()
    parts0 = {(0, 0): tile3[...]}
    for i, offset in enumerate(BALL):
        parts0[offset] = ghost3[i]
    once, parts1 = {}, {}
    for i, at in enumerate(NEXT):
        once[at] = sweep(parts0[at], parts0[at], extend(parts0, at), i)
        parts1[at] = jnp.where(lane < 64, once[at], take(once[at], qlane_ref[i]))
    c2 = [sweep(once[at], parts0[at], extend(parts1, at), i) for i, at in enumerate(NEAR)]
    corr_ref[...] = c2[0][:, :64]
    sources = (
        jnp.where(lane < 64, c2[0], pltpu.roll(c2[1], 64, 1)),
        jnp.where(lane < 64, c2[2], pltpu.roll(c2[3], 64, 1)),
        c2[4],
    )
    for f in range(FACES + 1):
        for t in range(GROUPS):
            span = slice(t * 128, (t + 1) * 128)
            row = codes_ref[(f + 6) % 7 : (f + 6) % 7 + 1, span]
            index = jnp.broadcast_to((row >> 3) & 127, (8, 128))
            group = jnp.broadcast_to(row >> 10, (8, 128))
            kid = jnp.broadcast_to(row & 7, (8, 128))
            kid = jnp.where(jnp.broadcast_to(row, (8, 128)) < 0, -1, kid)
            picked = jnp.zeros((8, 128), F32)
            for s in range(3 if f else 1):
                picked = jnp.where(group == s, take(sources[s], index), picked)
            if f:
                weight = face_scale_ref[f - 1 : f, span] * (omega * inverse)[:, span]
                picked = -weight * picked
            high, low = halves(picked)
            d_hi[f * 64 : (f + 1) * 64, span] = jnp.concatenate(
                [jnp.where(kid == k, high, 0.0) for k in range(8)], axis=0
            ).astype(BF16)
            d_lo[f * 64 : (f + 1) * 64, span] = jnp.concatenate(
                [jnp.where(kid == k, low, 0.0) for k in range(8)], axis=0
            ).astype(BF16)
    both = bf_dot(final_ref[...], d_hi[...])
    rest = bf_dot(final_ref[:64], d_lo[...])
    out_ref[...] = base_ref[...] + (both[:64] + both[64:] + rest)
    for group in (first, second, third):
        for copy in group:
            copy.wait_send()


def body(wide, narrow, *args):
    (
        start_field,
        right_side,
        element_scale,
        face_scale,
        face_nbr,
        send_list,
        counts,
        coarse_slot,
        elem_block,
        smooth_block,
        face_blocks,
        prolong,
        coarse_scale,
        coarse_face_scale,
        coarse_nbr,
        coarse_send,
        coarse_block,
        coarse_smooth,
        coarse_faces,
    ) = args
    vmem = pl.BlockSpec(memory_space=pltpu.VMEM)
    specs = [pl.BlockSpec(memory_space=pltpu.HBM)] * len(args)
    return tuple(
        pl.pallas_call(
            functools.partial(kernel, wide, narrow),
            out_shape=[
                pltpu.VMEM((64, 512), F32),
                pltpu.VMEM((8, 64), F32),
            ],
            in_specs=specs,
            out_specs=[vmem, vmem],
            scratch_shapes=[
                pltpu.VMEM((64, 512), F32),
                pltpu.VMEM((64, 768), F32),
                pltpu.VMEM((64, 512), F32),
                pltpu.VMEM((448, 768), F32),
                pltpu.VMEM((448, 192), BF16),
                pltpu.VMEM((448, 192), BF16),
                pltpu.VMEM((128, 192), BF16),
                pltpu.VMEM((448, 64), F32),
                pltpu.VMEM((448, 64), F32),
                pltpu.VMEM((128, 448), BF16),
                pltpu.VMEM((448, 512), BF16),
                pltpu.VMEM((448, 512), BF16),
                pltpu.VMEM((64, 512), F32),
                pltpu.VMEM((128, 512), F32),
                pltpu.VMEM((56, 8, 128), F32),
                pltpu.VMEM((128, 512), BF16),
                pltpu.VMEM((8, 512), jnp.int32),
                pltpu.VMEM((4, 40, 128), F32),
                pltpu.VMEM((4, 40, 128), F32),
                pltpu.VMEM((2, 56, 128), F32),
                pltpu.VMEM((2, 56, 128), F32),
                pltpu.VMEM((2, 40, 128), F32),
                pltpu.VMEM((2, 40, 128), F32),
                pltpu.VMEM((8, 128), F32),
                pltpu.VMEM((24, 8, 128), F32),
                pltpu.VMEM((13, 8, 128), jnp.int32),
                pltpu.VMEM((13, 8, 128), F32),
                pltpu.VMEM((13, 8, 128), jnp.int32),
                pltpu.SemaphoreType.DMA((2, 4)),
                pltpu.SemaphoreType.DMA((2, 4)),
                pltpu.SemaphoreType.DMA((24,)),
                pltpu.SemaphoreType.DMA((24,)),
                pltpu.VMEM((64, 512), F32),
                pltpu.VMEM((64, 512), F32),
                pltpu.VMEM((1, 512), F32),
                pltpu.VMEM((6, 512), F32),
                pltpu.VMEM((6, 512), jnp.int32),
                pltpu.VMEM((4, 64), jnp.int32),
                pltpu.VMEM((1, 512), jnp.int32),
                pltpu.VMEM((64, 64), F32),
                pltpu.VMEM((64, 64), F32),
                pltpu.VMEM((6, 64, 64), F32),
                pltpu.VMEM((64, 64), F32),
                pltpu.VMEM((1, 64), F32),
                pltpu.VMEM((6, 64), F32),
                pltpu.VMEM((6, 64), jnp.int32),
                pltpu.VMEM((4, 16), jnp.int32),
                pltpu.VMEM((8, 8), F32),
                pltpu.VMEM((8, 8), F32),
                pltpu.VMEM((6, 8, 8), F32),
                pltpu.SMEM((1, 1), jnp.int32),
                pltpu.SemaphoreType.DMA((19,)),
            ],
            compiler_params=pltpu.CompilerParams(
                collective_id=0, has_side_effects=True, vmem_limit_bytes=60 * 1024 * 1024
            ),
        )(
            start_field,
            right_side,
            element_scale.reshape(1, -1),
            face_scale,
            face_nbr,
            send_list,
            counts.reshape(1, 1),
            coarse_slot.reshape(1, -1),
            elem_block,
            smooth_block,
            face_blocks,
            prolong.transpose(0, 2, 1).reshape(64, 64),
            coarse_scale.reshape(1, -1),
            coarse_face_scale,
            coarse_nbr,
            coarse_send,
            coarse_block,
            coarse_smooth,
            coarse_faces,
        )
    )


def solution(mesh):
    both = ("wide", "narrow")
    split1, split2, whole = P(both), P(None, both), P()
    return jax.shard_map(
        functools.partial(body, mesh.shape["wide"], mesh.shape["narrow"]),
        mesh=mesh,
        in_specs=(
            split2,
            split2,
            split1,
            split2,
            split2,
            split2,
            split1,
            split1,
            whole,
            whole,
            whole,
            whole,
            split1,
            split2,
            split2,
            split2,
            whole,
            whole,
            whole,
        ),
        out_specs=(split2, split2),
        check_vma=False,
    )
```

```python
import functools

import jax
import jax.numpy as jnp
from jax import lax
from jax.experimental import pallas as pl
from jax.experimental.pallas import tpu as pltpu
from jax.sharding import PartitionSpec as P

OMEGA = 0.7
COARSE_OMEGA = 0.6
HIGH = lax.Precision.HIGHEST
F32 = jnp.float32
BF16 = jnp.bfloat16
FACES = 6
GROUPS = 4
NT = (((1,), (1,)), ((), ()))
SOURCES = ((-1, 0), (1, 0), (0, -1), (0, 1))
RANGE = range(-3, 4)
BALL = sorted(
    ((a, b) for a in RANGE for b in RANGE if 0 < abs(a) + abs(b) <= 3),
    key=lambda o: (-abs(o[0]) - abs(o[1]), o),
)
NEAR = ((0, 0),) + SOURCES
NEXT = NEAR + ((-2, 0), (-1, -1), (-1, 1), (2, 0), (1, -1), (1, 1), (0, -2), (0, 2))


def take(values, lanes):
    return jnp.take_along_axis(values, lanes, axis=1, mode="promise_in_bounds")


def halves(x):
    high = x.astype(BF16).astype(F32)
    return high, x - high


def exact_dot(a, b):
    return jnp.dot(a, b, preferred_element_type=F32, precision=HIGH)


def stack_left(a):
    high, low = halves(a)
    return jnp.concatenate([high, low, high], axis=1).astype(BF16)


def stack_right(b):
    high, low = halves(b)
    high = high.astype(BF16)
    return jnp.concatenate([high, high, low.astype(BF16)], axis=0)


def bf_dot(a, b):
    return jnp.dot(a, b, preferred_element_type=F32)


def kernel(
    wide,
    narrow,
    start_hbm,
    right_hbm,
    scale_hbm,
    face_scale_hbm,
    nbr_hbm,
    send_hbm,
    counts_hbm,
    slot_hbm,
    elem_hbm,
    smooth_hbm,
    faces_hbm,
    prolong_hbm,
    cscale_hbm,
    cface_scale_hbm,
    cnbr_hbm,
    csend_hbm,
    cblock_hbm,
    csmooth_hbm,
    cfaces_hbm,
    out_ref,
    corr_ref,
    x_ref,
    sm_ref,
    n_ref,
    y_ref,
    lhs_s,
    lhs_p,
    lhs_sp,
    comp_s,
    comp_p,
    final_ref,
    d_hi,
    d_lo,
    base_ref,
    t_ref,
    coef_ref,
    sent_ref,
    sent_ghost,
    sent_weight,
    child_ghost,
    child_weight,
    codes_ref,
    pack1,
    ghost1,
    pack2,
    ghost2,
    pack2n,
    ghost2n,
    tile3,
    ghost3,
    clane_ref,
    cweight_ref,
    qlane_ref,
    send_sem,
    recv_sem,
    send_sem3,
    recv_sem3,
    start_ref,
    right_ref,
    scale_ref,
    face_scale_ref,
    nbr_ref,
    send_ref,
    slot_ref,
    elem_ref,
    smooth_ref,
    faces_ref,
    prolong_ref,
    cscale_ref,
    cface_scale_ref,
    cnbr_ref,
    csend_ref,
    cblock_ref,
    csmooth_ref,
    cfaces_ref,
    counts_ref,
    load_sem,
):
    loads = {
        name: pltpu.make_async_copy(source, target, load_sem.at[i])
        for i, (name, source, target) in enumerate(
            (
                ("send", send_hbm, send_ref),
                ("counts", counts_hbm, counts_ref),
                ("start", start_hbm, start_ref),
                ("slot", slot_hbm, slot_ref),
                ("right", right_hbm, right_ref),
                ("scale", scale_hbm, scale_ref),
                ("face_scale", face_scale_hbm, face_scale_ref),
                ("nbr", nbr_hbm, nbr_ref),
                ("elem", elem_hbm, elem_ref),
                ("smooth", smooth_hbm, smooth_ref),
                ("faces", faces_hbm, faces_ref),
                ("prolong", prolong_hbm, prolong_ref),
                ("cscale", cscale_hbm, cscale_ref),
                ("cface_scale", cface_scale_hbm, cface_scale_ref),
                ("cnbr", cnbr_hbm, cnbr_ref),
                ("csend", csend_hbm, csend_ref),
                ("cblock", cblock_hbm, cblock_ref),
                ("csmooth", csmooth_hbm, csmooth_ref),
                ("cfaces", cfaces_hbm, cfaces_ref),
            )
        )
    }
    for load in loads.values():
        load.start()

    def arrive(*names):
        for name in names:
            loads[name].wait()

    me_w = lax.axis_index("wide")
    me_n = lax.axis_index("narrow")
    targets = (
        {"wide": lax.rem(me_w + 1, wide), "narrow": me_n},
        {"wide": lax.rem(me_w + wide - 1, wide), "narrow": me_n},
        {"wide": me_w, "narrow": lax.rem(me_n + 1, narrow)},
        {"wide": me_w, "narrow": lax.rem(me_n + narrow - 1, narrow)},
    )
    barrier = pltpu.get_barrier_semaphore()
    for target in targets:
        pl.semaphore_signal(
            barrier, inc=1, device_id=target, device_id_type=pl.DeviceIdType.MESH
        )

    lane = lax.broadcasted_iota(jnp.int32, (8, 128), 1)
    lane1 = lax.broadcasted_iota(jnp.int32, (1, 128), 1)
    low32 = jnp.broadcast_to(lane1 < 64, (32, 128))
    element = lax.broadcasted_iota(jnp.int32, (1, 512), 1)

    def copies(step, sources, buffers):
        return [
            pltpu.make_async_remote_copy(
                src_ref=sources[d],
                dst_ref=buffers[d],
                send_sem=send_sem.at[step, d],
                recv_sem=recv_sem.at[step, d],
                device_id=targets[d],
                device_id_type=pl.DeviceIdType.MESH,
            )
            for d in range(4)
        ]

    def start_all(group):
        for d in (2, 3, 0, 1):
            group[d].start()

    def send_row(pair):
        return jnp.concatenate(
            [send_ref[2 * pair : 2 * pair + 1, :], send_ref[2 * pair + 1 : 2 * pair + 2, :]], axis=1
        )

    def at_sends(pair, groups):
        rows = groups[0].shape[0]
        row = send_row(pair)
        index = jnp.broadcast_to(row & 127, (rows, 128))
        group = jnp.broadcast_to(row >> 7, (rows, 128))
        picked = jnp.zeros((rows, 128), F32)
        for s in range(GROUPS):
            picked = jnp.where(group == s, take(groups[s], index), picked)
        return picked

    def lane_groups(x):
        return [x[:, s * 128 : (s + 1) * 128] for s in range(GROUPS)]

    def fill(pair, picked, packets):
        moved = pltpu.roll(picked[32:], 64, 1)
        packets[2 * pair][0:32, :] = jnp.where(low32, picked[:32], moved)
        packets[2 * pair + 1][0:32, :] = jnp.where(low32, moved, picked[:32])

    def from_ghosts(rows, row):
        index = jnp.broadcast_to(row & 127, (rows.stop - rows.start, 128))
        second = jnp.broadcast_to(row >= 128, (rows.stop - rows.start, 128))
        return jnp.where(second, take(y_ref[rows, 640:768], index), take(y_ref[rows, 512:640], index))

    def unpack(ghosts):
        columns = []
        for pair in range(2):
            a = ghosts[2 * pair][0:32, :]
            b = ghosts[2 * pair + 1][0:32, :]
            first = jnp.where(low32, a, b)
            second = pltpu.roll(jnp.where(low32, b, a), 64, 1)
            columns.append(jnp.concatenate([first, second], axis=0))
        return jnp.concatenate(columns, axis=1)

    def gather_faces(groups, fresh):
        for t in range(GROUPS):
            span = slice(t * 128, (t + 1) * 128)
            total = jnp.zeros((64, 128), F32) if fresh else n_ref[:, span]
            for f in range(FACES):
                row = nbr_ref[f : f + 1, span]
                index = jnp.broadcast_to(row & 127, (64, 128))
                group = jnp.broadcast_to(row >> 7, (64, 128))
                picked = jnp.zeros((64, 128), F32)
                for s in groups:
                    got = take(
                        y_ref[(f + 1) * 64 : (f + 2) * 64, s * 128 : (s + 1) * 128], index
                    )
                    picked = jnp.where(group == s, got, picked)
                total = total + face_scale_ref[f : f + 1, span] * picked
            n_ref[:, span] = total

    arrive("counts", "send", "start", "slot", "cscale", "cface_scale", "cnbr", "csend")
    active = jnp.where(element < counts_ref[0, 0], 1.0, 0.0).astype(F32)
    x_ref[...] = start_ref[...] * active
    codes = jnp.where(active > 0.0, slot_ref[...].astype(F32), -1.0)
    cinv = COARSE_OMEGA / jnp.concatenate([cscale_ref[...]] * 2, axis=1)
    cnbr = cnbr_ref[...]
    weights = jnp.where(cnbr >= 0, cface_scale_ref[...], 0.0) * cinv[:, :64]
    csend = csend_ref[...]
    static = jnp.concatenate(
        [
            jnp.concatenate([jnp.maximum(cnbr, 0).astype(F32), weights], axis=1),
            jnp.concatenate([csend[d : d + 1] for d in range(4)] * 2, axis=1).astype(F32),
        ],
        axis=0,
    )
    for pair in range(2):
        fill(pair, at_sends(pair, lane_groups(x_ref)), [pack1.at[d] for d in range(4)])
        picked = at_sends(pair, [jnp.broadcast_to(c, (8, 128)) for c in lane_groups(codes)])
        tile = jnp.concatenate([static, picked[:1]], axis=0)
        pack1[2 * pair, 32:40, :] = tile
        pack1[2 * pair + 1, 32:40, :] = tile
    pl.semaphore_wait(barrier, 4)
    first = copies(0, [pack1.at[d] for d in range(4)], [ghost1.at[d] for d in range(4)])
    start_all(first)

    arrive("smooth", "elem", "faces", "nbr", "face_scale", "csmooth", "prolong", "right", "scale")
    smooth = smooth_ref[...]
    csmooth = csmooth_ref[...]
    prolong_t = prolong_ref[...]
    for f in range(FACES + 1):
        block = elem_ref[...] if f == 0 else faces_ref[f - 1]
        comp_s[f * 64 : (f + 1) * 64, :] = exact_dot(smooth, block)
    lhs_s[...] = stack_left(comp_s[...])
    y_ref[:, :512] = bf_dot(lhs_s[...], stack_right(x_ref[...]))
    gather_faces(range(GROUPS), True)
    row_blocks = lax.broadcasted_iota(jnp.int32, (64, 64), 0) >> 3
    column_blocks = lax.broadcasted_iota(jnp.int32, (64, 64), 1) >> 3
    tiled = jnp.concatenate([csmooth] * 8, axis=1)
    tiled = jnp.concatenate([tiled] * 8, axis=0)
    diagonal = jnp.where(row_blocks == column_blocks, tiled, 0.0)
    restrict = exact_dot(diagonal, prolong_t)
    lhs_sp[...] = stack_left(jnp.concatenate([smooth, restrict], axis=0))
    t_ref[...] = bf_dot(lhs_sp[...], stack_right(right_ref[...]))
    inverse = 1.0 / scale_ref[...]
    omega = OMEGA * active

    step = -omega * inverse
    sm_ref[:, :512] = x_ref[...] + omega * (t_ref[:64] * inverse - y_ref[:64, :512]) + step * n_ref[...]
    nbr = nbr_ref[...]
    remote = nbr >= 512
    ghost = jnp.where(remote, nbr - 512, 0).astype(F32)
    weight = jnp.where(remote, face_scale_ref[...], 0.0)
    blank = jnp.zeros((2, 512), F32)
    ghost = jnp.concatenate([ghost, blank], axis=0)
    weight = jnp.concatenate([weight, blank], axis=0)
    for pair in range(2):
        span = slice(pair * 128, (pair + 1) * 128)
        sent_ref[:, span] = at_sends(pair, lane_groups(sm_ref))
        sent_ghost[:, span] = at_sends(pair, lane_groups(ghost)).astype(jnp.int32)
        sent_weight[:, span] = at_sends(pair, lane_groups(step * weight))
    slot = slot_ref[...]
    place = (slot & 7) * 64 + (slot >> 3)
    order = jnp.where(lax.broadcasted_iota(jnp.int32, (512, 512), 0) == place, 1.0, 0.0).astype(BF16)
    high, rest = halves(weight)
    middle, low = halves(rest)
    tables = jnp.concatenate([ghost, high, middle, low], axis=0).astype(BF16)
    ordered = lax.dot_general(tables, order, NT, preferred_element_type=F32)
    child_ghost[...] = ordered[:8].astype(jnp.int32)
    child_weight[...] = ordered[8:16] + (ordered[16:24] + ordered[24:])

    for copy in first:
        copy.wait_recv()
    y_ref[64:, 512:] = bf_dot(lhs_s[64:, :], stack_right(unpack([ghost1.at[d] for d in range(4)])))
    packets2 = [pack2.at[0], pack2.at[1], pack2n.at[0], pack2n.at[1]]
    arrived2 = [ghost2.at[0], ghost2.at[1], ghost2n.at[0], ghost2n.at[1]]
    for d in range(4):
        for i, source in enumerate((d, 2, 3) if d < 2 else (d,)):
            packets2[d][32 + 8 * i : 40 + 8 * i, :] = ghost1[source, 32:40, :]
    for pair in range(2):
        span = slice(pair * 128, (pair + 1) * 128)
        total = sent_ref[:, span]
        for f in range(FACES):
            found = from_ghosts(slice((f + 1) * 64, (f + 2) * 64), sent_ghost[f : f + 1, span])
            total = total + sent_weight[f : f + 1, span] * found
        fill(pair, total, packets2)
    second = copies(1, packets2, arrived2)
    start_all(second)

    gather_faces((4, 5), True)
    sm_ref[:, :512] = sm_ref[:, :512] + step * n_ref[...]
    for f in range(FACES + 1):
        block = elem_ref[...] if f == 0 else faces_ref[f - 1]
        comp_p[f * 64 : (f + 1) * 64, :] = exact_dot(restrict, block)
    lhs_p[...] = stack_left(comp_p[...])
    y_ref[:, :512] = bf_dot(lhs_p[...], stack_right(sm_ref[:, :512]))
    gather_faces(range(GROUPS), True)
    n_ref[...] = active * t_ref[64:] - scale_ref[...] * y_ref[:64, :512] - n_ref[...]
    child = slot & 7
    chosen = jnp.zeros((8, 512), F32)
    for k in range(8):
        chosen = jnp.where(child == k, n_ref[8 * k : 8 * k + 8, :], chosen)
    row128 = lax.broadcasted_iota(jnp.int32, (128, 512), 0) & 63
    onehot = jnp.where(row128 == (slot >> 3), 1.0, 0.0).astype(BF16)
    high, low = halves(chosen)
    both = jnp.concatenate([high, low], axis=0).astype(BF16)
    summed = lax.dot_general(both, onehot, NT, preferred_element_type=F32)
    local_c = summed[:8] + summed[8:]
    arrive("cblock", "cfaces")
    together = jnp.concatenate([cblock_ref[...]] + [cfaces_ref[f] for f in range(FACES)], axis=1)
    coarse = exact_dot(csmooth, together)
    for c in range(8 * (FACES + 1)):
        coef_ref[c] = jnp.broadcast_to(coarse[:, c : c + 1], (8, 128))

    def keep_static(i, tile):
        clane_ref[i] = tile.astype(jnp.int32)
        cweight_ref[i] = pltpu.roll(tile, 64, 1)
        qlane_ref[i] = jnp.broadcast_to(tile[6:7], (8, 128)).astype(jnp.int32)

    keep_static(0, pack1[0, 32:40, :])
    for d in range(4):
        keep_static(1 + d, ghost1[d, 32:40, :])

    for copy in second:
        copy.wait_recv()
    sm_ref[:, 512:] = unpack(arrived2)
    y_ref[64:, 512:] = bf_dot(lhs_p[64:, :], stack_right(sm_ref[:, 512:]))

    ghost_c = jnp.zeros((8, 128), F32)
    for t in range(GROUPS):
        span = slice(t * 128, (t + 1) * 128)
        for f in range(FACES):
            at = (f + 1) * 64 + 16 * t
            row = child_ghost[f : f + 1, span]
            even = from_ghosts(slice(at, at + 8), row)
            odd = from_ghosts(slice(at + 8, at + 16), row)
            ghost_c = ghost_c + child_weight[f : f + 1, span] * jnp.where(lane < 64, even, odd)
    base_c = (local_c - (ghost_c + pltpu.roll(ghost_c, 64, 1))) * cinv

    def extend(parts, at):
        ext = parts[at]
        for d, (a, b) in enumerate(SOURCES):
            here = (lane >= 64 + 16 * d) & (lane < 80 + 16 * d)
            ext = jnp.where(here, parts[(at[0] + a, at[1] + b)], ext)
        return ext

    def sweep(own, right, ext, i):
        rows = [jnp.broadcast_to(ext[j : j + 1, :], (8, 128)) for j in range(8)]
        total = None
        for f in range(FACES + 1):
            product = coef_ref[8 * f] * rows[0]
            for j in range(1, 8):
                product = product + coef_ref[8 * f + j] * rows[j]
            if f == 0:
                total = COARSE_OMEGA * product
            else:
                index = jnp.broadcast_to(clane_ref[i, f - 1 : f, :], (8, 128))
                total = total + cweight_ref[i, f - 1 : f, :] * take(product, index)
        return own + right - total

    tile3[...] = jnp.where(lane < 64, base_c, take(base_c, qlane_ref[0]))
    third = [
        pltpu.make_async_remote_copy(
            src_ref=tile3,
            dst_ref=ghost3.at[BALL.index((-a, -b))],
            send_sem=send_sem3.at[i],
            recv_sem=recv_sem3.at[BALL.index((-a, -b))],
            device_id={
                "wide": lax.rem(me_w + (a + wide), wide),
                "narrow": lax.rem(me_n + (b + narrow), narrow),
            },
            device_id_type=pl.DeviceIdType.MESH,
        )
        for i, (a, b) in enumerate(BALL)
    ]
    for copy in third:
        copy.start()

    y_ref[...] = bf_dot(lhs_s[...], stack_right(sm_ref[...]))
    gather_faces(range(GROUPS), True)
    eye = jnp.where(
        lax.broadcasted_iota(jnp.int32, (64, 64), 0) == lax.broadcasted_iota(jnp.int32, (64, 64), 1),
        1.0,
        0.0,
    )
    left = jnp.concatenate([eye - OMEGA * comp_s[:64], comp_s[64:]], axis=0)
    products = lax.dot_general(left, prolong_t, NT, preferred_element_type=F32, precision=HIGH)
    wide_products = jnp.concatenate(
        [products[f * 64 : (f + 1) * 64] for f in range(FACES + 1)], axis=1
    )
    high, low = halves(wide_products)
    final_ref[...] = jnp.concatenate([high, low], axis=0).astype(BF16)

    for d in range(2):
        for i in range(3):
            keep_static(5 + 3 * d + i, ghost2[d, 32 + 8 * i : 40 + 8 * i, :])
        keep_static(11 + d, ghost2n[d, 32:40, :])
    gather_faces((4, 5), False)
    base_ref[...] = sm_ref[:, :512] + omega * (
        (t_ref[:64] - n_ref[...]) * inverse - y_ref[:64, :512]
    )
    code_groups = [
        jnp.broadcast_to(codes[:, s * 128 : (s + 1) * 128], (8, 128)) for s in range(GROUPS)
    ]
    for pair in range(2):
        a = jnp.broadcast_to(ghost1[2 * pair, 39:40, :], (8, 128))
        b = jnp.broadcast_to(ghost1[2 * pair + 1, 39:40, :], (8, 128))
        a = jnp.where(a >= 0.0, a + 512.0 * (2 * pair + 1), -1.0)
        b = jnp.where(b >= 0.0, b + 512.0 * (2 * pair + 2), -1.0)
        code_groups.append(jnp.where(lane < 64, a, b))
    for t in range(GROUPS):
        span = slice(t * 128, (t + 1) * 128)
        table = jnp.concatenate([nbr_ref[:, span], jnp.full((2, 128), -1, jnp.int32)], axis=0)
        index = table & 127
        group = table >> 7
        picked = jnp.full((8, 128), -1.0, F32)
        for s in range(GROUPS + 2):
            picked = jnp.where(group == s, take(code_groups[s], index), picked)
        codes_ref[:, span] = picked.astype(jnp.int32)
    codes_ref[6:7, :] = codes.astype(jnp.int32)

    for copy in third:
        copy.wait_recv()
    parts0 = {(0, 0): tile3[...]}
    for i, offset in enumerate(BALL):
        parts0[offset] = ghost3[i]
    once, parts1 = {}, {}
    for i, at in enumerate(NEXT):
        once[at] = sweep(parts0[at], parts0[at], extend(parts0, at), i)
        parts1[at] = jnp.where(lane < 64, once[at], take(once[at], qlane_ref[i]))
    c2 = [sweep(once[at], parts0[at], extend(parts1, at), i) for i, at in enumerate(NEAR)]
    corr_ref[...] = c2[0][:, :64]
    sources = (
        jnp.where(lane < 64, c2[0], pltpu.roll(c2[1], 64, 1)),
        jnp.where(lane < 64, c2[2], pltpu.roll(c2[3], 64, 1)),
        c2[4],
    )
    for f in range(FACES + 1):
        for t in range(GROUPS):
            span = slice(t * 128, (t + 1) * 128)
            row = codes_ref[(f + 6) % 7 : (f + 6) % 7 + 1, span]
            index = jnp.broadcast_to((row >> 3) & 127, (8, 128))
            group = jnp.broadcast_to(row >> 10, (8, 128))
            kid = jnp.broadcast_to(row & 7, (8, 128))
            kid = jnp.where(jnp.broadcast_to(row, (8, 128)) < 0, -1, kid)
            picked = jnp.zeros((8, 128), F32)
            for s in range(3 if f else 1):
                picked = jnp.where(group == s, take(sources[s], index), picked)
            if f:
                weight = face_scale_ref[f - 1 : f, span] * (omega * inverse)[:, span]
                picked = -weight * picked
            high, low = halves(picked)
            d_hi[f * 64 : (f + 1) * 64, span] = jnp.concatenate(
                [jnp.where(kid == k, high, 0.0) for k in range(8)], axis=0
            ).astype(BF16)
            d_lo[f * 64 : (f + 1) * 64, span] = jnp.concatenate(
                [jnp.where(kid == k, low, 0.0) for k in range(8)], axis=0
            ).astype(BF16)
    both = bf_dot(final_ref[...], d_hi[...])
    rest = bf_dot(final_ref[:64], d_lo[...])
    out_ref[...] = base_ref[...] + (both[:64] + both[64:] + rest)
    for group in (first, second, third):
        for copy in group:
            copy.wait_send()


def body(wide, narrow, *args):
    (
        start_field,
        right_side,
        element_scale,
        face_scale,
        face_nbr,
        send_list,
        counts,
        coarse_slot,
        elem_block,
        smooth_block,
        face_blocks,
        prolong,
        coarse_scale,
        coarse_face_scale,
        coarse_nbr,
        coarse_send,
        coarse_block,
        coarse_smooth,
        coarse_faces,
    ) = args
    vmem = pl.BlockSpec(memory_space=pltpu.VMEM)
    specs = [pl.BlockSpec(memory_space=pltpu.HBM)] * len(args)
    return tuple(
        pl.pallas_call(
            functools.partial(kernel, wide, narrow),
            out_shape=[
                pltpu.VMEM((64, 512), F32),
                pltpu.VMEM((8, 64), F32),
            ],
            in_specs=specs,
            out_specs=[vmem, vmem],
            scratch_shapes=[
                pltpu.VMEM((64, 512), F32),
                pltpu.VMEM((64, 768), F32),
                pltpu.VMEM((64, 512), F32),
                pltpu.VMEM((448, 768), F32),
                pltpu.VMEM((448, 192), BF16),
                pltpu.VMEM((448, 192), BF16),
                pltpu.VMEM((128, 192), BF16),
                pltpu.VMEM((448, 64), F32),
                pltpu.VMEM((448, 64), F32),
                pltpu.VMEM((128, 448), BF16),
                pltpu.VMEM((448, 512), BF16),
                pltpu.VMEM((448, 512), BF16),
                pltpu.VMEM((64, 512), F32),
                pltpu.VMEM((128, 512), F32),
                pltpu.VMEM((56, 8, 128), F32),
                pltpu.VMEM((64, 256), F32),
                pltpu.VMEM((8, 256), jnp.int32),
                pltpu.VMEM((8, 256), F32),
                pltpu.VMEM((8, 512), jnp.int32),
                pltpu.VMEM((8, 512), F32),
                pltpu.VMEM((8, 512), jnp.int32),
                pltpu.VMEM((4, 40, 128), F32),
                pltpu.VMEM((4, 40, 128), F32),
                pltpu.VMEM((2, 56, 128), F32),
                pltpu.VMEM((2, 56, 128), F32),
                pltpu.VMEM((2, 40, 128), F32),
                pltpu.VMEM((2, 40, 128), F32),
                pltpu.VMEM((8, 128), F32),
                pltpu.VMEM((24, 8, 128), F32),
                pltpu.VMEM((13, 8, 128), jnp.int32),
                pltpu.VMEM((13, 8, 128), F32),
                pltpu.VMEM((13, 8, 128), jnp.int32),
                pltpu.SemaphoreType.DMA((2, 4)),
                pltpu.SemaphoreType.DMA((2, 4)),
                pltpu.SemaphoreType.DMA((24,)),
                pltpu.SemaphoreType.DMA((24,)),
                pltpu.VMEM((64, 512), F32),
                pltpu.VMEM((64, 512), F32),
                pltpu.VMEM((1, 512), F32),
                pltpu.VMEM((6, 512), F32),
                pltpu.VMEM((6, 512), jnp.int32),
                pltpu.VMEM((4, 64), jnp.int32),
                pltpu.VMEM((1, 512), jnp.int32),
                pltpu.VMEM((64, 64), F32),
                pltpu.VMEM((64, 64), F32),
                pltpu.VMEM((6, 64, 64), F32),
                pltpu.VMEM((64, 64), F32),
                pltpu.VMEM((1, 64), F32),
                pltpu.VMEM((6, 64), F32),
                pltpu.VMEM((6, 64), jnp.int32),
                pltpu.VMEM((4, 16), jnp.int32),
                pltpu.VMEM((8, 8), F32),
                pltpu.VMEM((8, 8), F32),
                pltpu.VMEM((6, 8, 8), F32),
                pltpu.SMEM((1, 1), jnp.int32),
                pltpu.SemaphoreType.DMA((19,)),
            ],
            compiler_params=pltpu.CompilerParams(
                collective_id=0, has_side_effects=True, vmem_limit_bytes=60 * 1024 * 1024
            ),
        )(
            start_field,
            right_side,
            element_scale.reshape(1, -1),
            face_scale,
            face_nbr,
            send_list,
            counts.reshape(1, 1),
            coarse_slot.reshape(1, -1),
            elem_block,
            smooth_block,
            face_blocks,
            prolong.transpose(0, 2, 1).reshape(64, 64),
            coarse_scale.reshape(1, -1),
            coarse_face_scale,
            coarse_nbr,
            coarse_send,
            coarse_block,
            coarse_smooth,
            coarse_faces,
        )
    )


def solution(mesh):
    both = ("wide", "narrow")
    split1, split2, whole = P(both), P(None, both), P()
    return jax.shard_map(
        functools.partial(body, mesh.shape["wide"], mesh.shape["narrow"]),
        mesh=mesh,
        in_specs=(
            split2,
            split2,
            split1,
            split2,
            split2,
            split2,
            split1,
            split1,
            whole,
            whole,
            whole,
            whole,
            split1,
            split2,
            split2,
            split2,
            whole,
            whole,
            whole,
        ),
        out_specs=(split2, split2),
        check_vma=False,
    )
```
